32 devices in a mesh: group: 2 (over y), expert: 4 (over z), dp: 4 (over x, core).
Axes of the slice: x: 2, y: 2, z: 4, core: 2. Of those that a mesh axis runs over, the one named last changes fastest.
Arguments:
- grad_out: bfloat16 [4096, 2048], P(('group', 'expert', 'dp')), parts along dimension 0, may hold values from -6 to 6
- expert_ids: int32 [4096, 8], P(('group', 'expert', 'dp')), parts along dimension 0, may hold values from 0 to 15, all different within a row; in each aligned block of 128 rows (0 to 127, 128 to 255, ...) at most 128 rows name the same one
- probs: bfloat16 [4096, 8], P(('group', 'expert', 'dp')), parts along dimension 0, may hold values from 0.019897461 to 0.5
- hidden: bfloat16 [4096, 8, 384], P(('group', 'expert', 'dp')), parts along dimension 0, may hold values from -1.5 to 1.5
- weights: bfloat16 [16, 384, 2048], P(('expert', 'dp')), may hold values from -0.125 to 0.125
- momentum: bfloat16 [32, 384, 2048], P(('group', 'expert', 'dp')), parts along dimension 0, may hold values from -6 to 6
Outputs:
- grad_hidden: bfloat16 [4096, 8, 384], P(('group', 'expert', 'dp')), parts along dimension 0
- grad_prob: float32 [4096, 8], P(('group', 'expert', 'dp')), parts along dimension 0
- new_momentum: bfloat16 [32, 384, 2048], P(('group', 'expert', 'dp')), parts along dimension 0
- update: float32 [32, 384, 2048], P(('group', 'expert', 'dp')), parts along dimension 0
The draws below stay inside these ranges and needn't reach their ends.
There are 2 independent parts, one for each index of `group`. The reference program is written for one: setup_inputs(seed, part) draws one part's arguments, and reference() takes and returns one part's arrays. A program takes and returns all parts, laid end to end along the dimension named above; an argument that names none is the same for every part. Nothing has to cross between parts.
Inputs may be any that keep to these rules, and one draw needn't show every extreme that they name: `expert_ids`: each row names 8 different experts; among the 128 rows of one device no expert is named more than 128 times, and in every draw some expert is named exactly 128 times by some device.
All inputs are finite; a program needn't handle non-finite values.
Results may differ from the reference program's by a relative error of at most 0.04.
Values may be sent and summed in bfloat16 or wider, within the bound.
A program may use at most 128 MiB of HBM per device.

```python
import math
import jax
import jax.numpy as jnp
import numpy as np
from jax import lax

D = 2048
TOP = 8
F = 384
ITERS = 5
TOK_DEV = 128
EXPERTS = 16
TOKENS = 2048
CAP = 128
N_EXPERT = 4
N_DP = 4


def steps_of(stream_key, dims, pieces, low, high):
    factor_of = 1.0
    for position, parts in pieces:
        draws = jax.random.uniform(jax.random.fold_in(jax.random.fold_in(stream_key, 6), position), (parts,), jnp.float32, low / len(pieces), high / len(pieces))
        factor_of = factor_of * jnp.repeat(jnp.exp(draws), dims[position] // parts).reshape((-1,) + (1,) * (len(dims) - 1 - position))
    return factor_of


def deal_out(stream_key, own, number, rows, number_of, top, reach, lean):
    sequence = jax.random.permutation(stream_key, number_of)
    heavy_load, usual = portions_of(number_of, rows * top, reach, lean, True), portions_of(number_of, rows * top, reach, lean, False)
    places = jnp.arange(number_of)

    def named(lengths, offset_by):
        used = int((lengths > 0).sum())
        fixed = max(1, used // 4)
        moved = fixed + (places - fixed + offset_by * (used - fixed)) % max(1, number_of - fixed)
        return jnp.zeros((number_of,), jnp.int32).at[sequence[jnp.where(places < fixed, places, moved)]].set(jnp.asarray(lengths, jnp.int32))

    lengths = jnp.where(number % 4 == 0, named(heavy_load, number // 4), named(usual, number - number // 4 - 1))
    mixed = jax.random.permutation(jax.random.fold_in(own, 3), number_of)
    donor, taker = mixed[0:number_of // 2 * 2:2], mixed[1:number_of // 2 * 2:2]
    slack = jnp.minimum(lengths[donor] - 1, reach - lengths[taker]) // 2
    slack = jnp.where((donor == sequence[0]) | (taker == sequence[0]) | (lengths[taker] == 0), 0, jnp.maximum(slack, 0))
    moved = jax.random.randint(jax.random.fold_in(own, 4), (number_of // 2,), 0, 1 << 20) % (slack + 1)
    lengths = lengths.at[donor].add(-moved).at[taker].add(moved)
    labels = jnp.searchsorted(jnp.cumsum(lengths), jnp.arange(rows * top), side="right").astype(jnp.int32)
    listing = labels.reshape(top, rows).T
    listing = listing[jax.random.permutation(jax.random.fold_in(own, 1), rows)]
    offset_by = jax.random.randint(jax.random.fold_in(own, 2), (rows, 1), 0, top)
    return jnp.take_along_axis(listing, (jnp.arange(top)[None, :] + offset_by) % top, axis=1)


def portions_of(number_of, total, most, skew, full):
    weights = [(1 << 20) // math.isqrt(standing ** skew) + 1 for standing in range(1, number_of + 1)]
    largest = most if full else min(most, max(-(-total // number_of), total * weights[0] // sum(weights)))
    least = 1 if total - largest >= number_of - 1 else 0
    given, surplus = [largest] + [least] * (number_of - 1), total - largest - least * (number_of - 1)
    while surplus > 0:
        movable = [i for i in range(1, number_of) if given[i] < largest] or [i for i in range(1, number_of) if given[i] < most]
        mass, remaining = sum([weights[i] for i in movable]), surplus
        for i in movable:
            addition = min(most - given[i], max(1, remaining * weights[i] // mass), surplus)
            given[i] = given[i] + addition
            surplus = surplus - addition
    return np.array(given)


def gaussian(stream_key, dims, scale, limit, cuts=(), kind=jnp.bfloat16):
    drawn = jax.random.normal(stream_key, dims, jnp.float32) * scale
    if len(cuts) > 0:
        drawn = steps_of(stream_key, dims, cuts, -0.22, 0.18) * drawn
    return jnp.clip(drawn, min=-limit, max=limit).astype(kind)


def setup_inputs(seed: int = 0, part: int = 0) -> dict:
    seeds = jax.random.split(jax.random.key(seed), 7)
    part_keys = jax.random.split(jax.random.fold_in(seeds[6], part), 7)
    grad_out = gaussian(part_keys[0], (TOKENS, D), 1.0, 6.0, ((0, 16),))
    expert_ids_keys = jax.random.split(jax.random.fold_in(part_keys[1], 1), TOKENS // TOK_DEV)
    expert_ids_turns = jax.random.permutation(jax.random.fold_in(part_keys[1], 3), TOKENS // TOK_DEV)
    expert_ids = jax.vmap(lambda own, number: deal_out(jax.random.fold_in(part_keys[1], 2), own, number, TOK_DEV, EXPERTS, TOP, CAP, 2))(expert_ids_keys, expert_ids_turns).reshape((TOKENS, TOP))
    probs = jnp.clip(jnp.exp(math.log(0.5) - 3.224016 * jax.random.uniform(part_keys[2], (TOKENS, TOP), jnp.float32) ** steps_of(part_keys[2], (TOKENS, TOP), ((0, 16),), -0.2, 0.2)), 0.019897461, 0.5).astype(jnp.bfloat16)
    hidden = gaussian(part_keys[3], (TOKENS, TOP, F), 0.25, 1.5, ((0, 16),))
    weights = gaussian(seeds[4], (EXPERTS, F, D), D ** -0.5, 0.125, ((0, 16),))
    momentum = gaussian(part_keys[5], (EXPERTS, F, D), 1.0, 6.0, ((0, 16),))
    return dict(grad_out=grad_out, expert_ids=expert_ids, probs=probs, hidden=hidden, weights=weights, momentum=momentum)


momentum_decay = 0.95
coef_a = 3.4445
coef_b = -4.775
coef_c = 2.0315

def orthogonal(matrix):
    values = matrix.astype(jnp.float32)
    frob_norm = jnp.sqrt(jnp.sum(values * values))
    iterate = (values / (frob_norm + 1e-07)).astype(jnp.bfloat16)
    for step_index in range(ITERS):
        gram_matrix = jnp.dot(iterate, iterate.T, preferred_element_type=jnp.float32).astype(jnp.bfloat16)
        gram_square = jnp.dot(gram_matrix, gram_matrix, preferred_element_type=jnp.float32)
        poly_mix = (coef_b * gram_matrix.astype(jnp.float32) + coef_c * gram_square).astype(jnp.bfloat16)
        iterate = (coef_a * iterate.astype(jnp.float32) + jnp.dot(poly_mix, iterate, preferred_element_type=jnp.float32)).astype(jnp.bfloat16)
    return iterate.astype(jnp.float32) * math.sqrt(D)

def reference(grad_out, expert_ids, probs, hidden, weights, momentum):
    total_rows = TOKENS * TOP
    flat_ids = expert_ids.reshape(-1).astype(jnp.int32)
    sorted_rows = jnp.argsort(flat_ids, stable=True).astype(jnp.int32)
    onehot = (flat_ids[:, None] == jnp.arange(EXPERTS, dtype=jnp.int32)[None, :]).astype(jnp.int32)
    counts = lax.optimization_barrier(jnp.sum(onehot, 0)).astype(jnp.int32)
    starts = (jnp.cumsum(counts) - counts).astype(jnp.int32)
    row_limit = CAP * N_EXPERT * N_DP
    padded_rows = jnp.concatenate([sorted_rows, jnp.full((row_limit,), total_rows, jnp.int32)])
    hidden_flat = hidden.reshape(total_rows, F)
    hidden_pad = jnp.concatenate([hidden_flat, jnp.zeros((1, F), hidden.dtype)], 0)
    prob_pad = jnp.concatenate([probs.reshape(-1), jnp.zeros((1,), probs.dtype)])

    def per_expert(collected, expert_index):
        row_index = lax.dynamic_slice(padded_rows, (starts[expert_index],), (row_limit,))
        valid_rows = jnp.arange(row_limit, dtype=jnp.int32) < counts[expert_index]
        row_index = jnp.where(valid_rows, row_index, total_rows).astype(jnp.int32)
        token_index = jnp.minimum(row_index, total_rows - 1) // TOP
        grad_rows = jnp.where(valid_rows[:, None], grad_out[token_index], jnp.zeros((), grad_out.dtype))
        hid_rows = hidden_pad[row_index]
        prob_rows = prob_pad[row_index]
        matrix = weights[expert_index]
        raw_grad = jnp.dot(grad_rows, matrix.T, preferred_element_type=jnp.float32).astype(jnp.bfloat16)
        scaled = (prob_rows[:, None].astype(jnp.float32) * grad_rows.astype(jnp.float32)).astype(jnp.bfloat16)
        grad_weights = jnp.dot(hid_rows.T, scaled, preferred_element_type=jnp.float32)
        new_mom = (momentum_decay * momentum[expert_index].astype(jnp.float32) + grad_weights).astype(jnp.bfloat16)
        collected = collected.at[row_index].set(raw_grad)
        return (collected, (new_mom, orthogonal(new_mom)))
    start_raw = jnp.zeros((total_rows + 1, F), jnp.bfloat16)
    collected, stacked = lax.scan(per_expert, start_raw, jnp.arange(EXPERTS, dtype=jnp.int32))
    new_momentum, update = stacked
    raw_rows = collected[:total_rows]
    grad_hidden = (probs.reshape(-1)[:, None].astype(jnp.float32) * raw_rows.astype(jnp.float32)).astype(jnp.bfloat16)
    grad_prob = lax.optimization_barrier(jnp.sum(raw_rows.astype(jnp.float32) * hidden_flat.astype(jnp.float32), 1))
    return (grad_hidden.reshape(TOKENS, TOP, F), grad_prob.reshape(TOKENS, TOP), new_momentum, update)
```

```python
import math

import jax
import jax.numpy as jnp
from jax import lax
from jax.sharding import PartitionSpec as P

EXP_DEV = 4
ITERS = 5


momentum_decay = 0.95
coef_a = 3.4445
coef_b = -4.775
coef_c = 2.0315


def orthogonal(matrix):
    values = matrix.astype(jnp.float32)
    frob_norm = jnp.sqrt(jnp.sum(values * values))
    iterate = (values / (frob_norm + 1e-07)).astype(jnp.bfloat16)
    for step_index in range(ITERS):
        gram_matrix = jnp.dot(iterate, iterate.T, preferred_element_type=jnp.float32).astype(
            jnp.bfloat16
        )
        gram_square = jnp.dot(gram_matrix, gram_matrix, preferred_element_type=jnp.float32)
        poly_mix = (coef_b * gram_matrix.astype(jnp.float32) + coef_c * gram_square).astype(
            jnp.bfloat16
        )
        iterate = (
            coef_a * iterate.astype(jnp.float32)
            + jnp.dot(poly_mix, iterate, preferred_element_type=jnp.float32)
        ).astype(jnp.bfloat16)
    return iterate.astype(jnp.float32) * math.sqrt(matrix.shape[1])


def scale_rows(prob_slots, grad_slots):
    return (prob_slots[..., None].astype(jnp.float32) * grad_slots.astype(jnp.float32)).astype(
        jnp.bfloat16
    )


def shards(grad_out, expert_ids, probs, hidden, weights, momentum):
    tok_rows, model_width = grad_out.shape
    top_count = expert_ids.shape[1]
    hidden_width = hidden.shape[2]
    owner_count = lax.axis_size("expert")
    expert_total = EXP_DEV * owner_count
    capacity = 2 * tok_rows * top_count // expert_total
    routed_rows = tok_rows * top_count
    flat_ids = expert_ids.reshape(-1)
    onehot = (flat_ids[:, None] == jnp.arange(expert_total, dtype=jnp.int32)[None, :]).astype(
        jnp.int32
    )
    before = jnp.cumsum(onehot, 0) - onehot
    position_in = jnp.sum(before * onehot, 1)
    owner_rank = flat_ids // EXP_DEV
    local_index = flat_ids % EXP_DEV
    buffer_index = (local_index * owner_count + owner_rank) * capacity + position_in
    source_map = (
        jnp.zeros((expert_total * capacity,), jnp.int32)
        .at[buffer_index]
        .set(jnp.arange(routed_rows, dtype=jnp.int32) + 1)
    )
    filled = source_map > 0
    source_row = jnp.maximum(source_map - 1, 0)
    hidden_flat = hidden.reshape(routed_rows, hidden_width)
    prob_flat = probs.reshape(-1)
    zero_value = jnp.zeros((), jnp.bfloat16)
    send_grad = jnp.where(filled[:, None], grad_out[source_row // top_count], zero_value).reshape(
        EXP_DEV, owner_count, capacity, model_width
    )
    send_hidden = jnp.where(filled[:, None], hidden_flat[source_row], zero_value).reshape(
        EXP_DEV, owner_count, capacity, hidden_width
    )
    send_prob = jnp.where(filled, prob_flat[source_row], zero_value).reshape(
        EXP_DEV, owner_count, capacity
    )
    recv_grad, recv_hidden, recv_prob = (
        lax.all_to_all(send_grad, "expert", split_axis=1, concat_axis=1, tiled=True),
        lax.all_to_all(send_hidden, "expert", split_axis=1, concat_axis=1, tiled=True),
        lax.all_to_all(send_prob, "expert", split_axis=1, concat_axis=1, tiled=True),
    )
    grad_part = recv_grad
    raw_grad = jnp.einsum(
        "escd,efd->escf",
        grad_part,
        lax.all_gather(weights, "dp", axis=0, tiled=True),
        preferred_element_type=jnp.float32,
    ).astype(jnp.bfloat16)
    grad_part = recv_grad
    scaled = scale_rows(recv_prob, grad_part)
    grad_weights = lax.psum_scatter(
        jnp.einsum(
            "escf,escd->efd", recv_hidden, scaled, preferred_element_type=jnp.float32
        ).astype(jnp.bfloat16),
        "dp",
        scatter_dimension=0,
        tiled=True,
    ).astype(jnp.float32)
    returned = lax.all_to_all(raw_grad, "expert", split_axis=1, concat_axis=1, tiled=True)
    raw_rows = returned.reshape(expert_total * capacity, hidden_width)[buffer_index]
    grad_hidden = (prob_flat[:, None].astype(jnp.float32) * raw_rows.astype(jnp.float32)).astype(
        jnp.bfloat16
    )
    grad_prob = jnp.sum(raw_rows.astype(jnp.float32) * hidden_flat.astype(jnp.float32), 1)
    new_momentum = (momentum_decay * momentum.astype(jnp.float32) + grad_weights).astype(
        jnp.bfloat16
    )
    update = jax.vmap(orthogonal)(new_momentum)
    return (
        grad_hidden.reshape(tok_rows, top_count, hidden_width),
        grad_prob.reshape(tok_rows, top_count),
        new_momentum,
        update,
    )


def dense_shards(grad_out, expert_ids, probs, hidden, weights, momentum):
    axes = ("expert", "dp")
    tok_rows, model_width = grad_out.shape
    top_count = expert_ids.shape[1]
    hidden_width = hidden.shape[2]
    device_count = lax.axis_size("expert") * lax.axis_size("dp")
    expert_total = device_count * weights.shape[0]
    all_grad = lax.all_gather(grad_out, axes, axis=0, tiled=True)
    experts = jnp.arange(expert_total, dtype=jnp.int32)
    zero_value = jnp.zeros((), jnp.bfloat16)
    prob_hidden = (probs[..., None].astype(jnp.float32) * hidden.astype(jnp.float32)).astype(
        jnp.bfloat16
    )
    send_hidden = jnp.zeros((expert_total, tok_rows, hidden_width), jnp.bfloat16)
    for choice in range(top_count):
        named = expert_ids[None, :, choice] == experts[:, None]
        send_hidden = jnp.where(named[..., None], prob_hidden[None, :, choice], send_hidden)
    recv_hidden = lax.all_to_all(send_hidden, axes, split_axis=0, concat_axis=0, tiled=True)
    raw_grad = lax.dot_general(
        all_grad, weights[0], (((1,), (1,)), ((), ())), preferred_element_type=jnp.float32
    ).astype(jnp.bfloat16)
    returned = lax.all_to_all(
        raw_grad.reshape(device_count, tok_rows, hidden_width),
        axes,
        split_axis=0,
        concat_axis=0,
        tiled=True,
    )
    grad_weights = lax.dot_general(
        recv_hidden.reshape(device_count * tok_rows, hidden_width),
        all_grad,
        (((0,), (0,)), ((), ())),
        preferred_element_type=jnp.float32,
    )[None]
    new_momentum = (momentum_decay * momentum.astype(jnp.float32) + grad_weights).astype(
        jnp.bfloat16
    )
    update = jax.vmap(orthogonal)(new_momentum)
    raw_rows = jnp.zeros((tok_rows, top_count, hidden_width), jnp.bfloat16)
    for expert in range(expert_total):
        named = expert_ids == expert
        raw_rows = jnp.where(named[..., None], returned[expert][:, None], raw_rows)
    grad_hidden = (probs[..., None].astype(jnp.float32) * raw_rows.astype(jnp.float32)).astype(
        jnp.bfloat16
    )
    grad_prob = jnp.sum(raw_rows.astype(jnp.float32) * hidden.astype(jnp.float32), 2)
    return grad_hidden, grad_prob, new_momentum, update


def solution(mesh):
    in_specs = (
        P(("group", "expert", "dp"), None),
        P(("group", "expert", "dp"), None),
        P(("group", "expert", "dp"), None),
        P(("group", "expert", "dp"), None, None),
        P(("expert", "dp"), None, None),
        P(("group", "expert", "dp"), None, None),
    )
    out_specs = (
        P(("group", "expert", "dp"), None, None),
        P(("group", "expert", "dp"), None),
        P(("group", "expert", "dp"), None, None),
        P(("group", "expert", "dp"), None, None),
    )

    owners = mesh.shape["expert"]
    dp_count = mesh.shape["dp"]

    def program(grad_out, expert_ids, probs, hidden, weights, momentum):
        tok_rows = grad_out.shape[0] // (mesh.shape["group"] * owners * dp_count)
        expert_total = weights.shape[0]
        dense = expert_total == owners * dp_count and (
            2 * tok_rows * expert_ids.shape[1] // expert_total >= tok_rows
        )
        return jax.shard_map(
            dense_shards if dense else shards,
            mesh=mesh,
            in_specs=in_specs,
            out_specs=out_specs,
            check_vma=False,
        )(grad_out, expert_ids, probs, hidden, weights, momentum)

    return program
```

```python
import math

import jax
import jax.numpy as jnp
from jax import lax
from jax.sharding import PartitionSpec as P

EXP_DEV = 4
ITERS = 5


momentum_decay = 0.95
coef_a = 3.4445
coef_b = -4.775
coef_c = 2.0315


def orthogonal(matrix):
    values = matrix.astype(jnp.float32)
    frob_norm = jnp.sqrt(jnp.sum(values * values))
    iterate = (values / (frob_norm + 1e-07)).astype(jnp.bfloat16)
    for step_index in range(ITERS):
        gram_matrix = jnp.dot(iterate, iterate.T, preferred_element_type=jnp.float32).astype(
            jnp.bfloat16
        )
        gram_square = jnp.dot(gram_matrix, gram_matrix, preferred_element_type=jnp.float32)
        poly_mix = (coef_b * gram_matrix.astype(jnp.float32) + coef_c * gram_square).astype(
            jnp.bfloat16
        )
        iterate = (
            coef_a * iterate.astype(jnp.float32)
            + jnp.dot(poly_mix, iterate, preferred_element_type=jnp.float32)
        ).astype(jnp.bfloat16)
    return iterate.astype(jnp.float32) * math.sqrt(matrix.shape[1])


def scale_rows(prob_slots, grad_slots):
    return (prob_slots[..., None].astype(jnp.float32) * grad_slots.astype(jnp.float32)).astype(
        jnp.bfloat16
    )


def shards(grad_out, expert_ids, probs, hidden, weights, momentum):
    tok_rows, model_width = grad_out.shape
    top_count = expert_ids.shape[1]
    hidden_width = hidden.shape[2]
    owner_count = lax.axis_size("expert")
    expert_total = EXP_DEV * owner_count
    capacity = 2 * tok_rows * top_count // expert_total
    routed_rows = tok_rows * top_count
    flat_ids = expert_ids.reshape(-1)
    onehot = (flat_ids[:, None] == jnp.arange(expert_total, dtype=jnp.int32)[None, :]).astype(
        jnp.int32
    )
    before = jnp.cumsum(onehot, 0) - onehot
    position_in = jnp.sum(before * onehot, 1)
    owner_rank = flat_ids // EXP_DEV
    local_index = flat_ids % EXP_DEV
    buffer_index = (local_index * owner_count + owner_rank) * capacity + position_in
    source_map = (
        jnp.zeros((expert_total * capacity,), jnp.int32)
        .at[buffer_index]
        .set(jnp.arange(routed_rows, dtype=jnp.int32) + 1)
    )
    filled = source_map > 0
    source_row = jnp.maximum(source_map - 1, 0)
    hidden_flat = hidden.reshape(routed_rows, hidden_width)
    prob_flat = probs.reshape(-1)
    zero_value = jnp.zeros((), jnp.bfloat16)
    send_grad = jnp.where(filled[:, None], grad_out[source_row // top_count], zero_value).reshape(
        EXP_DEV, owner_count, capacity, model_width
    )
    send_hidden = jnp.where(filled[:, None], hidden_flat[source_row], zero_value).reshape(
        EXP_DEV, owner_count, capacity, hidden_width
    )
    send_prob = jnp.where(filled, prob_flat[source_row], zero_value).reshape(
        EXP_DEV, owner_count, capacity
    )
    recv_grad, recv_hidden, recv_prob = (
        lax.all_to_all(send_grad, "expert", split_axis=1, concat_axis=1, tiled=True),
        lax.all_to_all(send_hidden, "expert", split_axis=1, concat_axis=1, tiled=True),
        lax.all_to_all(send_prob, "expert", split_axis=1, concat_axis=1, tiled=True),
    )
    grad_part = recv_grad
    raw_grad = jnp.einsum(
        "escd,efd->escf",
        grad_part,
        lax.all_gather(weights, "dp", axis=0, tiled=True),
        preferred_element_type=jnp.float32,
    ).astype(jnp.bfloat16)
    grad_part = recv_grad
    scaled = scale_rows(recv_prob, grad_part)
    grad_weights = lax.psum_scatter(
        jnp.einsum(
            "escf,escd->efd", recv_hidden, scaled, preferred_element_type=jnp.float32
        ).astype(jnp.bfloat16),
        "dp",
        scatter_dimension=0,
        tiled=True,
    ).astype(jnp.float32)
    returned = lax.all_to_all(raw_grad, "expert", split_axis=1, concat_axis=1, tiled=True)
    raw_rows = returned.reshape(expert_total * capacity, hidden_width)[buffer_index]
    grad_hidden = (prob_flat[:, None].astype(jnp.float32) * raw_rows.astype(jnp.float32)).astype(
        jnp.bfloat16
    )
    grad_prob = jnp.sum(raw_rows.astype(jnp.float32) * hidden_flat.astype(jnp.float32), 1)
    new_momentum = (momentum_decay * momentum.astype(jnp.float32) + grad_weights).astype(
        jnp.bfloat16
    )
    update = jax.vmap(orthogonal)(new_momentum)
    return (
        grad_hidden.reshape(tok_rows, top_count, hidden_width),
        grad_prob.reshape(tok_rows, top_count),
        new_momentum,
        update,
    )


def dense_shards(grad_out, expert_ids, probs, hidden, weights, momentum):
    axes = ("expert", "dp")
    tok_rows, model_width = grad_out.shape
    top_count = expert_ids.shape[1]
    hidden_width = hidden.shape[2]
    device_count = lax.axis_size("expert") * lax.axis_size("dp")
    expert_total = device_count * weights.shape[0]
    all_grad = lax.all_gather(grad_out, axes, axis=0, tiled=True)
    experts = jnp.arange(expert_total, dtype=jnp.int32)
    zero_value = jnp.zeros((), jnp.bfloat16)
    prob_hidden = (probs[..., None].astype(jnp.float32) * hidden.astype(jnp.float32)).astype(
        jnp.bfloat16
    )
    send_hidden = jnp.zeros((expert_total, tok_rows, hidden_width), jnp.bfloat16)
    for choice in range(top_count):
        named = expert_ids[None, :, choice] == experts[:, None]
        send_hidden = jnp.where(named[..., None], prob_hidden[None, :, choice], send_hidden)
    recv_hidden = lax.all_to_all(send_hidden, axes, split_axis=0, concat_axis=0, tiled=True)
    all_grad, recv_hidden = lax.optimization_barrier((all_grad, recv_hidden))
    raw_grad = lax.dot_general(
        all_grad, weights[0], (((1,), (1,)), ((), ())), preferred_element_type=jnp.float32
    ).astype(jnp.bfloat16)
    raw_grad, recv_hidden = lax.optimization_barrier((raw_grad, recv_hidden))
    returned = lax.all_to_all(
        raw_grad.reshape(device_count, tok_rows, hidden_width),
        axes,
        split_axis=0,
        concat_axis=0,
        tiled=True,
    )
    grad_weights = lax.dot_general(
        recv_hidden.reshape(device_count * tok_rows, hidden_width),
        all_grad,
        (((0,), (0,)), ((), ())),
        preferred_element_type=jnp.float32,
    )[None]
    new_momentum = (momentum_decay * momentum.astype(jnp.float32) + grad_weights).astype(
        jnp.bfloat16
    )
    update = jax.vmap(orthogonal)(new_momentum)
    update, returned = lax.optimization_barrier((update, returned))
    raw_rows = jnp.zeros((tok_rows, top_count, hidden_width), jnp.bfloat16)
    for expert in range(expert_total):
        named = expert_ids == expert
        raw_rows = jnp.where(named[..., None], returned[expert][:, None], raw_rows)
    grad_hidden = (probs[..., None].astype(jnp.float32) * raw_rows.astype(jnp.float32)).astype(
        jnp.bfloat16
    )
    grad_prob = jnp.sum(raw_rows.astype(jnp.float32) * hidden.astype(jnp.float32), 2)
    return grad_hidden, grad_prob, new_momentum, update


def solution(mesh):
    in_specs = (
        P(("group", "expert", "dp"), None),
        P(("group", "expert", "dp"), None),
        P(("group", "expert", "dp"), None),
        P(("group", "expert", "dp"), None, None),
        P(("expert", "dp"), None, None),
        P(("group", "expert", "dp"), None, None),
    )
    out_specs = (
        P(("group", "expert", "dp"), None, None),
        P(("group", "expert", "dp"), None),
        P(("group", "expert", "dp"), None, None),
        P(("group", "expert", "dp"), None, None),
    )

    owners = mesh.shape["expert"]
    dp_count = mesh.shape["dp"]

    def program(grad_out, expert_ids, probs, hidden, weights, momentum):
        tok_rows = grad_out.shape[0] // (mesh.shape["group"] * owners * dp_count)
        expert_total = weights.shape[0]
        dense = expert_total == owners * dp_count and (
            2 * tok_rows * expert_ids.shape[1] // expert_total >= tok_rows
        )
        return jax.shard_map(
            dense_shards if dense else shards,
            mesh=mesh,
            in_specs=in_specs,
            out_specs=out_specs,
            check_vma=False,
        )(grad_out, expert_ids, probs, hidden, weights, momentum)

    return program
```

```python
import functools
import math

import jax
import jax.numpy as jnp
from jax import lax
from jax.experimental import pallas as pl
from jax.experimental.pallas import tpu as pltpu
from jax.sharding import PartitionSpec as P

EXP_DEV = 4
ITERS = 5


momentum_decay = 0.95
coef_a = 3.4445
coef_b = -4.775
coef_c = 2.0315


def orthogonal(matrix):
    values = matrix.astype(jnp.float32)
    frob_norm = jnp.sqrt(jnp.sum(values * values))
    iterate = (values / (frob_norm + 1e-07)).astype(jnp.bfloat16)
    for step_index in range(ITERS):
        gram_matrix = jnp.dot(iterate, iterate.T, preferred_element_type=jnp.float32).astype(
            jnp.bfloat16
        )
        gram_square = jnp.dot(gram_matrix, gram_matrix, preferred_element_type=jnp.float32)
        poly_mix = (coef_b * gram_matrix.astype(jnp.float32) + coef_c * gram_square).astype(
            jnp.bfloat16
        )
        iterate = (
            coef_a * iterate.astype(jnp.float32)
            + jnp.dot(poly_mix, iterate, preferred_element_type=jnp.float32)
        ).astype(jnp.bfloat16)
    return iterate.astype(jnp.float32) * math.sqrt(matrix.shape[1])


def scale_rows(prob_slots, grad_slots):
    return (prob_slots[..., None].astype(jnp.float32) * grad_slots.astype(jnp.float32)).astype(
        jnp.bfloat16
    )


def shards(grad_out, expert_ids, probs, hidden, weights, momentum):
    tok_rows, model_width = grad_out.shape
    top_count = expert_ids.shape[1]
    hidden_width = hidden.shape[2]
    owner_count = lax.axis_size("expert")
    expert_total = EXP_DEV * owner_count
    capacity = 2 * tok_rows * top_count // expert_total
    routed_rows = tok_rows * top_count
    flat_ids = expert_ids.reshape(-1)
    onehot = (flat_ids[:, None] == jnp.arange(expert_total, dtype=jnp.int32)[None, :]).astype(
        jnp.int32
    )
    before = jnp.cumsum(onehot, 0) - onehot
    position_in = jnp.sum(before * onehot, 1)
    owner_rank = flat_ids // EXP_DEV
    local_index = flat_ids % EXP_DEV
    buffer_index = (local_index * owner_count + owner_rank) * capacity + position_in
    source_map = (
        jnp.zeros((expert_total * capacity,), jnp.int32)
        .at[buffer_index]
        .set(jnp.arange(routed_rows, dtype=jnp.int32) + 1)
    )
    filled = source_map > 0
    source_row = jnp.maximum(source_map - 1, 0)
    hidden_flat = hidden.reshape(routed_rows, hidden_width)
    prob_flat = probs.reshape(-1)
    zero_value = jnp.zeros((), jnp.bfloat16)
    send_grad = jnp.where(filled[:, None], grad_out[source_row // top_count], zero_value).reshape(
        EXP_DEV, owner_count, capacity, model_width
    )
    send_hidden = jnp.where(filled[:, None], hidden_flat[source_row], zero_value).reshape(
        EXP_DEV, owner_count, capacity, hidden_width
    )
    send_prob = jnp.where(filled, prob_flat[source_row], zero_value).reshape(
        EXP_DEV, owner_count, capacity
    )
    recv_grad, recv_hidden, recv_prob = (
        lax.all_to_all(send_grad, "expert", split_axis=1, concat_axis=1, tiled=True),
        lax.all_to_all(send_hidden, "expert", split_axis=1, concat_axis=1, tiled=True),
        lax.all_to_all(send_prob, "expert", split_axis=1, concat_axis=1, tiled=True),
    )
    grad_part = recv_grad
    raw_grad = jnp.einsum(
        "escd,efd->escf",
        grad_part,
        lax.all_gather(weights, "dp", axis=0, tiled=True),
        preferred_element_type=jnp.float32,
    ).astype(jnp.bfloat16)
    grad_part = recv_grad
    scaled = scale_rows(recv_prob, grad_part)
    grad_weights = lax.psum_scatter(
        jnp.einsum(
            "escf,escd->efd", recv_hidden, scaled, preferred_element_type=jnp.float32
        ).astype(jnp.bfloat16),
        "dp",
        scatter_dimension=0,
        tiled=True,
    ).astype(jnp.float32)
    returned = lax.all_to_all(raw_grad, "expert", split_axis=1, concat_axis=1, tiled=True)
    raw_rows = returned.reshape(expert_total * capacity, hidden_width)[buffer_index]
    grad_hidden = (prob_flat[:, None].astype(jnp.float32) * raw_rows.astype(jnp.float32)).astype(
        jnp.bfloat16
    )
    grad_prob = jnp.sum(raw_rows.astype(jnp.float32) * hidden_flat.astype(jnp.float32), 1)
    new_momentum = (momentum_decay * momentum.astype(jnp.float32) + grad_weights).astype(
        jnp.bfloat16
    )
    update = jax.vmap(orthogonal)(new_momentum)
    return (
        grad_hidden.reshape(tok_rows, top_count, hidden_width),
        grad_prob.reshape(tok_rows, top_count),
        new_momentum,
        update,
    )


def exchange_kernel(
    owners,
    width,
    grad_ref,
    hid_ref,
    all_ref,
    recv_ref,
    local_sem,
    up_sem,
    down_sem,
    cross_sem,
    sib_sem,
    block_sem,
    hid_send,
    hid_recv,
):
    total = owners * width
    row = lax.axis_index("expert")
    lane = lax.axis_index("dp")
    sibling = lane + 1 - 2 * lax.rem(lane, 2)
    cross = lax.rem(lane + 2, width)
    cross_sibling = lax.rem(sibling + 2, width)
    me = row * width + lane

    def target(peer_row, peer_lane):
        return {"expert": peer_row, "dp": peer_lane}

    def peer_at(offset):
        return lax.rem(me + offset, total)

    barrier = pltpu.get_barrier_semaphore()

    @pl.loop(1, total)
    def _(offset):
        peer = peer_at(offset)
        pl.semaphore_signal(
            barrier,
            inc=1,
            device_id=target(peer // width, lax.rem(peer, width)),
            device_id_type=pl.DeviceIdType.MESH,
        )

    pl.semaphore_wait(barrier, total - 1)

    def block_copy(source_row, source_lane, send_sem, peer_row, peer_lane, first=False):
        rank = source_row * width + source_lane
        return pltpu.make_async_remote_copy(
            src_ref=grad_ref if first else all_ref.at[rank],
            dst_ref=all_ref.at[rank],
            send_sem=send_sem,
            recv_sem=block_sem.at[rank],
            device_id=target(peer_row, peer_lane),
            device_id_type=pl.DeviceIdType.MESH,
        )

    def up(source_row, first=False):
        return block_copy(source_row, lane, up_sem.at[source_row], row + 1, lane, first)

    def down(source_row, first=False):
        return block_copy(source_row, lane, down_sem.at[source_row], row - 1, lane, first)

    def over(source_row, first=False):
        return block_copy(source_row, lane, cross_sem.at[source_row], row, cross, first)

    def aside(source_row, column, first=False):
        source_lane = cross if column else lane
        return block_copy(
            source_row, source_lane, sib_sem.at[source_row * 2 + column], row, sibling, first
        )

    def arrive(source_row, source_lane):
        block_copy(source_row, source_lane, up_sem.at[0], row, sibling).wait_recv()

    def hid_copy(offset):
        peer = peer_at(offset)
        return pltpu.make_async_remote_copy(
            src_ref=hid_ref.at[peer],
            dst_ref=recv_ref.at[me],
            send_sem=hid_send.at[offset],
            recv_sem=hid_recv.at[me],
            device_id=target(peer // width, lax.rem(peer, width)),
            device_id_type=pl.DeviceIdType.MESH,
        )

    @pl.when(row < owners - 1)
    def _():
        up(row, True).start()

    @pl.when(row > 0)
    def _():
        down(row, True).start()

    over(row, True).start()
    aside(row, 0, True).start()
    own_grad = pltpu.make_async_copy(grad_ref, all_ref.at[me], local_sem.at[0])
    own_grad.start()
    own_hid = pltpu.make_async_copy(hid_ref.at[me], recv_ref.at[me], local_sem.at[1])
    own_hid.start()

    @pl.loop(1, total)
    def _(offset):
        hid_copy(offset).start()

    def cross_arrival(source_row):
        arrive(source_row, cross)
        aside(source_row, 1).start()

    for step in range(1, owners + 1):
        if step < owners:

            @pl.when(row - step >= 0)
            def _():
                arrive(row - step, lane)

                @pl.when(row < owners - 1)
                def _():
                    up(row - step).start()

                over(row - step).start()
                aside(row - step, 0).start()

            @pl.when(row + step < owners)
            def _():
                arrive(row + step, lane)

                @pl.when(row > 0)
                def _():
                    down(row + step).start()

                over(row + step).start()
                aside(row + step, 0).start()

        if step == 1:
            cross_arrival(row)
        else:

            @pl.when(row - (step - 1) >= 0)
            def _():
                cross_arrival(row - (step - 1))

            @pl.when(row + (step - 1) < owners)
            def _():
                cross_arrival(row + (step - 1))

    own_grad.wait()
    own_hid.wait()

    @pl.loop(0, owners)
    def _(source_row):
        arrive(source_row, sibling)
        arrive(source_row, cross_sibling)
        over(source_row).wait_send()
        aside(source_row, 0).wait_send()
        aside(source_row, 1).wait_send()

        @pl.when((source_row <= row) & (row < owners - 1))
        def _():
            up(source_row).wait_send()

        @pl.when((source_row >= row) & (row > 0))
        def _():
            down(source_row).wait_send()

    @pl.loop(1, total)
    def _(offset):
        hid_copy(offset).wait_send()
        peer = peer_at(offset)
        pltpu.make_async_remote_copy(
            src_ref=hid_ref.at[peer],
            dst_ref=recv_ref.at[peer],
            send_sem=hid_send.at[offset],
            recv_sem=hid_recv.at[peer],
            device_id=target(peer // width, lax.rem(peer, width)),
            device_id_type=pl.DeviceIdType.MESH,
        ).wait_recv()


def exchange(grad_out, send_hidden):
    owners, width = lax.axis_size("expert"), lax.axis_size("dp")
    total = owners * width
    dma = pltpu.SemaphoreType.DMA
    return pl.pallas_call(
        functools.partial(exchange_kernel, owners, width),
        out_shape=(
            jax.ShapeDtypeStruct((total,) + grad_out.shape, grad_out.dtype),
            jax.ShapeDtypeStruct(send_hidden.shape, send_hidden.dtype),
        ),
        in_specs=[pl.BlockSpec(memory_space=pl.ANY)] * 2,
        out_specs=(pl.BlockSpec(memory_space=pl.ANY),) * 2,
        scratch_shapes=[
            dma((2,)),
            dma((owners,)),
            dma((owners,)),
            dma((owners,)),
            dma((2 * owners,)),
            dma((total,)),
            dma((total,)),
            dma((total,)),
        ],
        compiler_params=pltpu.CompilerParams(collective_id=0, has_side_effects=True),
        name="exchange",
    )(grad_out, send_hidden)


def dense_shards(grad_out, expert_ids, probs, hidden, weights, momentum):
    axes = ("expert", "dp")
    tok_rows, model_width = grad_out.shape
    top_count = expert_ids.shape[1]
    hidden_width = hidden.shape[2]
    device_count = lax.axis_size("expert") * lax.axis_size("dp")
    expert_total = device_count * weights.shape[0]
    experts = jnp.arange(expert_total, dtype=jnp.int32)
    zero_value = jnp.zeros((), jnp.bfloat16)
    prob_hidden = (probs[..., None].astype(jnp.float32) * hidden.astype(jnp.float32)).astype(
        jnp.bfloat16
    )
    send_hidden = jnp.zeros((expert_total, tok_rows, hidden_width), jnp.bfloat16)
    for choice in range(top_count):
        named = expert_ids[None, :, choice] == experts[:, None]
        send_hidden = jnp.where(named[..., None], prob_hidden[None, :, choice], send_hidden)
    all_grad, recv_hidden = exchange(grad_out, send_hidden)
    all_grad = all_grad.reshape(device_count * tok_rows, model_width)
    raw_grad = lax.dot_general(
        all_grad, weights[0], (((1,), (1,)), ((), ())), preferred_element_type=jnp.float32
    ).astype(jnp.bfloat16)
    returned = lax.all_to_all(
        raw_grad.reshape(device_count, tok_rows, hidden_width),
        axes,
        split_axis=0,
        concat_axis=0,
        tiled=True,
    )
    grad_weights = lax.dot_general(
        recv_hidden.reshape(device_count * tok_rows, hidden_width),
        all_grad,
        (((0,), (0,)), ((), ())),
        preferred_element_type=jnp.float32,
    )[None]
    new_momentum = (momentum_decay * momentum.astype(jnp.float32) + grad_weights).astype(
        jnp.bfloat16
    )
    update = jax.vmap(orthogonal)(new_momentum)
    update, returned = lax.optimization_barrier((update, returned))
    raw_rows = jnp.zeros((tok_rows, top_count, hidden_width), jnp.bfloat16)
    for expert in range(expert_total):
        named = expert_ids == expert
        raw_rows = jnp.where(named[..., None], returned[expert][:, None], raw_rows)
    grad_hidden = (probs[..., None].astype(jnp.float32) * raw_rows.astype(jnp.float32)).astype(
        jnp.bfloat16
    )
    grad_prob = jnp.sum(raw_rows.astype(jnp.float32) * hidden.astype(jnp.float32), 2)
    return grad_hidden, grad_prob, new_momentum, update


def solution(mesh):
    in_specs = (
        P(("group", "expert", "dp"), None),
        P(("group", "expert", "dp"), None),
        P(("group", "expert", "dp"), None),
        P(("group", "expert", "dp"), None, None),
        P(("expert", "dp"), None, None),
        P(("group", "expert", "dp"), None, None),
    )
    out_specs = (
        P(("group", "expert", "dp"), None, None),
        P(("group", "expert", "dp"), None),
        P(("group", "expert", "dp"), None, None),
        P(("group", "expert", "dp"), None, None),
    )

    owners = mesh.shape["expert"]
    dp_count = mesh.shape["dp"]

    def program(grad_out, expert_ids, probs, hidden, weights, momentum):
        tok_rows = grad_out.shape[0] // (mesh.shape["group"] * owners * dp_count)
        expert_total = weights.shape[0]
        dense = dp_count == 4 and expert_total == owners * dp_count and (
            2 * tok_rows * expert_ids.shape[1] // expert_total >= tok_rows
        )
        return jax.shard_map(
            dense_shards if dense else shards,
            mesh=mesh,
            in_specs=in_specs,
            out_specs=out_specs,
            check_vma=False,
        )(grad_out, expert_ids, probs, hidden, weights, momentum)

    return program
```

```python
import functools
import math

import jax
import jax.numpy as jnp
from jax import lax
from jax.experimental import pallas as pl
from jax.experimental.pallas import tpu as pltpu
from jax.sharding import PartitionSpec as P

EXP_DEV = 4
ITERS = 5


momentum_decay = 0.95
coef_a = 3.4445
coef_b = -4.775
coef_c = 2.0315


def orthogonal(matrix):
    values = matrix.astype(jnp.float32)
    frob_norm = jnp.sqrt(jnp.sum(values * values))
    iterate = (values / (frob_norm + 1e-07)).astype(jnp.bfloat16)
    for step_index in range(ITERS):
        gram_matrix = jnp.dot(iterate, iterate.T, preferred_element_type=jnp.float32).astype(
            jnp.bfloat16
        )
        gram_square = jnp.dot(gram_matrix, gram_matrix, preferred_element_type=jnp.float32)
        poly_mix = (coef_b * gram_matrix.astype(jnp.float32) + coef_c * gram_square).astype(
            jnp.bfloat16
        )
        iterate = (
            coef_a * iterate.astype(jnp.float32)
            + jnp.dot(poly_mix, iterate, preferred_element_type=jnp.float32)
        ).astype(jnp.bfloat16)
    return iterate.astype(jnp.float32) * math.sqrt(matrix.shape[1])


def scale_rows(prob_slots, grad_slots):
    return (prob_slots[..., None].astype(jnp.float32) * grad_slots.astype(jnp.float32)).astype(
        jnp.bfloat16
    )


def shards(grad_out, expert_ids, probs, hidden, weights, momentum):
    tok_rows, model_width = grad_out.shape
    top_count = expert_ids.shape[1]
    hidden_width = hidden.shape[2]
    owner_count = lax.axis_size("expert")
    expert_total = EXP_DEV * owner_count
    capacity = 2 * tok_rows * top_count // expert_total
    routed_rows = tok_rows * top_count
    flat_ids = expert_ids.reshape(-1)
    onehot = (flat_ids[:, None] == jnp.arange(expert_total, dtype=jnp.int32)[None, :]).astype(
        jnp.int32
    )
    before = jnp.cumsum(onehot, 0) - onehot
    position_in = jnp.sum(before * onehot, 1)
    owner_rank = flat_ids // EXP_DEV
    local_index = flat_ids % EXP_DEV
    buffer_index = (local_index * owner_count + owner_rank) * capacity + position_in
    source_map = (
        jnp.zeros((expert_total * capacity,), jnp.int32)
        .at[buffer_index]
        .set(jnp.arange(routed_rows, dtype=jnp.int32) + 1)
    )
    filled = source_map > 0
    source_row = jnp.maximum(source_map - 1, 0)
    hidden_flat = hidden.reshape(routed_rows, hidden_width)
    prob_flat = probs.reshape(-1)
    zero_value = jnp.zeros((), jnp.bfloat16)
    send_grad = jnp.where(filled[:, None], grad_out[source_row // top_count], zero_value).reshape(
        EXP_DEV, owner_count, capacity, model_width
    )
    send_hidden = jnp.where(filled[:, None], hidden_flat[source_row], zero_value).reshape(
        EXP_DEV, owner_count, capacity, hidden_width
    )
    send_prob = jnp.where(filled, prob_flat[source_row], zero_value).reshape(
        EXP_DEV, owner_count, capacity
    )
    recv_grad, recv_hidden, recv_prob = (
        lax.all_to_all(send_grad, "expert", split_axis=1, concat_axis=1, tiled=True),
        lax.all_to_all(send_hidden, "expert", split_axis=1, concat_axis=1, tiled=True),
        lax.all_to_all(send_prob, "expert", split_axis=1, concat_axis=1, tiled=True),
    )
    grad_part = recv_grad
    raw_grad = jnp.einsum(
        "escd,efd->escf",
        grad_part,
        lax.all_gather(weights, "dp", axis=0, tiled=True),
        preferred_element_type=jnp.float32,
    ).astype(jnp.bfloat16)
    grad_part = recv_grad
    scaled = scale_rows(recv_prob, grad_part)
    grad_weights = lax.psum_scatter(
        jnp.einsum(
            "escf,escd->efd", recv_hidden, scaled, preferred_element_type=jnp.float32
        ).astype(jnp.bfloat16),
        "dp",
        scatter_dimension=0,
        tiled=True,
    ).astype(jnp.float32)
    returned = lax.all_to_all(raw_grad, "expert", split_axis=1, concat_axis=1, tiled=True)
    raw_rows = returned.reshape(expert_total * capacity, hidden_width)[buffer_index]
    grad_hidden = (prob_flat[:, None].astype(jnp.float32) * raw_rows.astype(jnp.float32)).astype(
        jnp.bfloat16
    )
    grad_prob = jnp.sum(raw_rows.astype(jnp.float32) * hidden_flat.astype(jnp.float32), 1)
    new_momentum = (momentum_decay * momentum.astype(jnp.float32) + grad_weights).astype(
        jnp.bfloat16
    )
    update = jax.vmap(orthogonal)(new_momentum)
    return (
        grad_hidden.reshape(tok_rows, top_count, hidden_width),
        grad_prob.reshape(tok_rows, top_count),
        new_momentum,
        update,
    )


def exchange_kernel(
    owners,
    width,
    grad_ref,
    hid_ref,
    all_ref,
    recv_ref,
    local_sem,
    up_sem,
    down_sem,
    cross_sem,
    sib_sem,
    block_sem,
    hid_send,
    hid_recv,
):
    total = owners * width
    row = lax.axis_index("expert")
    lane = lax.axis_index("dp")
    sibling = lane + 1 - 2 * lax.rem(lane, 2)
    cross = lax.rem(lane + 2, width)
    cross_sibling = lax.rem(sibling + 2, width)
    me = row * width + lane

    def target(peer_row, peer_lane):
        return {"expert": peer_row, "dp": peer_lane}

    def peer_at(offset):
        return lax.rem(me + offset, total)

    barrier = pltpu.get_barrier_semaphore()

    @pl.loop(1, total)
    def _(offset):
        peer = peer_at(offset)
        pl.semaphore_signal(
            barrier,
            inc=1,
            device_id=target(peer // width, lax.rem(peer, width)),
            device_id_type=pl.DeviceIdType.MESH,
        )

    pl.semaphore_wait(barrier, total - 1)

    def block_copy(source_row, source_lane, send_sem, peer_row, peer_lane, first=False):
        rank = source_row * width + source_lane
        return pltpu.make_async_remote_copy(
            src_ref=grad_ref if first else all_ref.at[rank],
            dst_ref=all_ref.at[rank],
            send_sem=send_sem,
            recv_sem=block_sem.at[rank],
            device_id=target(peer_row, peer_lane),
            device_id_type=pl.DeviceIdType.MESH,
        )

    def up(source_row, first=False):
        return block_copy(source_row, lane, up_sem.at[source_row], row + 1, lane, first)

    def down(source_row, first=False):
        return block_copy(source_row, lane, down_sem.at[source_row], row - 1, lane, first)

    def over(source_row, first=False):
        return block_copy(source_row, lane, cross_sem.at[source_row], row, cross, first)

    def aside(source_row, column, first=False):
        source_lane = cross if column else lane
        return block_copy(
            source_row, source_lane, sib_sem.at[source_row * 2 + column], row, sibling, first
        )

    def arrive(source_row, source_lane):
        block_copy(source_row, source_lane, up_sem.at[0], row, sibling).wait_recv()

    def hid_copy(offset):
        peer = peer_at(offset)
        return pltpu.make_async_remote_copy(
            src_ref=hid_ref.at[peer],
            dst_ref=recv_ref.at[me],
            send_sem=hid_send.at[offset],
            recv_sem=hid_recv.at[me],
            device_id=target(peer // width, lax.rem(peer, width)),
            device_id_type=pl.DeviceIdType.MESH,
        )

    @pl.when(row < owners - 1)
    def _():
        up(row, True).start()

    @pl.when(row > 0)
    def _():
        down(row, True).start()

    over(row, True).start()
    aside(row, 0, True).start()
    own_grad = pltpu.make_async_copy(grad_ref, all_ref.at[me], local_sem.at[0])
    own_grad.start()
    own_hid = pltpu.make_async_copy(hid_ref.at[me], recv_ref.at[me], local_sem.at[1])
    own_hid.start()

    def start_hidden(low, high):
        @pl.loop(low, high)
        def _(offset):
            hid_copy(offset).start()

    first_batch = 1 + (total - 1) // 3

    def cross_arrival(source_row):
        arrive(source_row, cross)
        aside(source_row, 1).start()

    for step in range(1, owners + 1):
        if step < owners:

            @pl.when(row - step >= 0)
            def _():
                arrive(row - step, lane)

                @pl.when(row < owners - 1)
                def _():
                    up(row - step).start()

                over(row - step).start()
                aside(row - step, 0).start()

            @pl.when(row + step < owners)
            def _():
                arrive(row + step, lane)

                @pl.when(row > 0)
                def _():
                    down(row + step).start()

                over(row + step).start()
                aside(row + step, 0).start()

        if step == 1:
            start_hidden(1, first_batch)
        elif step == 2:
            start_hidden(first_batch, total)

        if step == 1:
            cross_arrival(row)
        else:

            @pl.when(row - (step - 1) >= 0)
            def _():
                cross_arrival(row - (step - 1))

            @pl.when(row + (step - 1) < owners)
            def _():
                cross_arrival(row + (step - 1))

    own_grad.wait()
    own_hid.wait()

    @pl.loop(0, owners)
    def _(source_row):
        arrive(source_row, sibling)
        arrive(source_row, cross_sibling)
        over(source_row).wait_send()
        aside(source_row, 0).wait_send()
        aside(source_row, 1).wait_send()

        @pl.when((source_row <= row) & (row < owners - 1))
        def _():
            up(source_row).wait_send()

        @pl.when((source_row >= row) & (row > 0))
        def _():
            down(source_row).wait_send()

    @pl.loop(1, total)
    def _(offset):
        hid_copy(offset).wait_send()
        peer = peer_at(offset)
        pltpu.make_async_remote_copy(
            src_ref=hid_ref.at[peer],
            dst_ref=recv_ref.at[peer],
            send_sem=hid_send.at[offset],
            recv_sem=hid_recv.at[peer],
            device_id=target(peer // width, lax.rem(peer, width)),
            device_id_type=pl.DeviceIdType.MESH,
        ).wait_recv()


def exchange(grad_out, send_hidden):
    owners, width = lax.axis_size("expert"), lax.axis_size("dp")
    total = owners * width
    dma = pltpu.SemaphoreType.DMA
    return pl.pallas_call(
        functools.partial(exchange_kernel, owners, width),
        out_shape=(
            jax.ShapeDtypeStruct((total,) + grad_out.shape, grad_out.dtype),
            jax.ShapeDtypeStruct(send_hidden.shape, send_hidden.dtype),
        ),
        in_specs=[pl.BlockSpec(memory_space=pl.ANY)] * 2,
        out_specs=(pl.BlockSpec(memory_space=pl.ANY),) * 2,
        scratch_shapes=[
            dma((2,)),
            dma((owners,)),
            dma((owners,)),
            dma((owners,)),
            dma((2 * owners,)),
            dma((total,)),
            dma((total,)),
            dma((total,)),
        ],
        compiler_params=pltpu.CompilerParams(collective_id=0, has_side_effects=True),
        name="exchange",
    )(grad_out, send_hidden)


def orthogonal_kernel(tiles, momentum_ref, update_ref, iterate_ref):
    height, width = momentum_ref.shape
    columns = width // tiles

    def tile(index):
        return pl.ds(pl.multiple_of(index * columns, columns), columns)

    def add_squares(index, total):
        values = momentum_ref[:, tile(index)].astype(jnp.float32)
        return total + jnp.sum(values * values, axis=0, keepdims=True)

    squares = lax.fori_loop(0, tiles, add_squares, jnp.zeros((1, columns), jnp.float32))
    frob_norm = jnp.sqrt(jnp.sum(squares, axis=1, keepdims=True)) + 1e-07

    @pl.loop(0, tiles)
    def _(index):
        values = momentum_ref[:, tile(index)].astype(jnp.float32)
        iterate_ref[:, tile(index)] = (values / frob_norm).astype(jnp.bfloat16)

    @pl.loop(0, ITERS)
    def _(step_index):
        iterate = iterate_ref[...]
        gram_matrix = lax.dot_general(
            iterate, iterate, (((1,), (1,)), ((), ())), preferred_element_type=jnp.float32
        ).astype(jnp.bfloat16)
        gram_square = jnp.dot(gram_matrix, gram_matrix, preferred_element_type=jnp.float32)
        poly_mix = (coef_b * gram_matrix.astype(jnp.float32) + coef_c * gram_square).astype(
            jnp.bfloat16
        )
        for index in range(tiles):
            part = pl.ds(index * columns, columns)
            block = iterate_ref[:, part]
            iterate_ref[:, part] = (
                coef_a * block.astype(jnp.float32)
                + jnp.dot(poly_mix, block, preferred_element_type=jnp.float32)
            ).astype(jnp.bfloat16)

    @pl.loop(0, tiles)
    def _(index):
        update_ref[:, tile(index)] = iterate_ref[:, tile(index)].astype(jnp.float32) * math.sqrt(
            width
        )


def orthogonal_block(matrix):
    height, width = matrix.shape
    macs = ITERS * height * height * (2 * width + height)
    return pl.pallas_call(
        functools.partial(orthogonal_kernel, width // 512),
        out_shape=jax.ShapeDtypeStruct(matrix.shape, jnp.float32),
        in_specs=[pl.BlockSpec(memory_space=pltpu.VMEM)],
        out_specs=pl.BlockSpec(memory_space=pltpu.VMEM),
        scratch_shapes=[pltpu.VMEM(matrix.shape, jnp.bfloat16)],
        compiler_params=pltpu.CompilerParams(vmem_limit_bytes=24 * 2**20),
        cost_estimate=pl.CostEstimate(
            flops=2 * macs, bytes_accessed=6 * height * width, transcendentals=0
        ),
        name="orthogonal",
    )(matrix)


def dense_shards(grad_out, expert_ids, probs, hidden, weights, momentum):
    axes = ("expert", "dp")
    tok_rows, model_width = grad_out.shape
    top_count = expert_ids.shape[1]
    hidden_width = hidden.shape[2]
    device_count = lax.axis_size("expert") * lax.axis_size("dp")
    expert_total = device_count * weights.shape[0]
    experts = jnp.arange(expert_total, dtype=jnp.int32)
    zero_value = jnp.zeros((), jnp.bfloat16)
    prob_hidden = (probs[..., None].astype(jnp.float32) * hidden.astype(jnp.float32)).astype(
        jnp.bfloat16
    )
    send_hidden = jnp.zeros((expert_total, tok_rows, hidden_width), jnp.bfloat16)
    for choice in range(top_count):
        named = expert_ids[None, :, choice] == experts[:, None]
        send_hidden = jnp.where(named[..., None], prob_hidden[None, :, choice], send_hidden)
    all_grad, recv_hidden = exchange(grad_out, send_hidden)
    all_grad = all_grad.reshape(device_count * tok_rows, model_width)
    raw_grad = lax.dot_general(
        all_grad, weights[0], (((1,), (1,)), ((), ())), preferred_element_type=jnp.float32
    ).astype(jnp.bfloat16)
    returned = lax.all_to_all(
        raw_grad.reshape(device_count, tok_rows, hidden_width),
        axes,
        split_axis=0,
        concat_axis=0,
        tiled=True,
    )
    grad_weights = lax.dot_general(
        recv_hidden.reshape(device_count * tok_rows, hidden_width),
        all_grad,
        (((0,), (0,)), ((), ())),
        preferred_element_type=jnp.float32,
    )[None]
    new_momentum = (momentum_decay * momentum.astype(jnp.float32) + grad_weights).astype(
        jnp.bfloat16
    )
    update = orthogonal_block(new_momentum[0])[None]
    update, returned = lax.optimization_barrier((update, returned))
    raw_rows = jnp.zeros((tok_rows, top_count, hidden_width), jnp.bfloat16)
    for expert in range(expert_total):
        named = expert_ids == expert
        raw_rows = jnp.where(named[..., None], returned[expert][:, None], raw_rows)
    grad_hidden = (probs[..., None].astype(jnp.float32) * raw_rows.astype(jnp.float32)).astype(
        jnp.bfloat16
    )
    grad_prob = jnp.sum(raw_rows.astype(jnp.float32) * hidden.astype(jnp.float32), 2)
    return grad_hidden, grad_prob, new_momentum, update


def solution(mesh):
    in_specs = (
        P(("group", "expert", "dp"), None),
        P(("group", "expert", "dp"), None),
        P(("group", "expert", "dp"), None),
        P(("group", "expert", "dp"), None, None),
        P(("expert", "dp"), None, None),
        P(("group", "expert", "dp"), None, None),
    )
    out_specs = (
        P(("group", "expert", "dp"), None, None),
        P(("group", "expert", "dp"), None),
        P(("group", "expert", "dp"), None, None),
        P(("group", "expert", "dp"), None, None),
    )

    owners = mesh.shape["expert"]
    dp_count = mesh.shape["dp"]

    def program(grad_out, expert_ids, probs, hidden, weights, momentum):
        tok_rows = grad_out.shape[0] // (mesh.shape["group"] * owners * dp_count)
        expert_total = weights.shape[0]
        dense = owners >= 3 and dp_count == 4 and expert_total == owners * dp_count and (
            2 * tok_rows * expert_ids.shape[1] // expert_total >= tok_rows
        )
        return jax.shard_map(
            dense_shards if dense else shards,
            mesh=mesh,
            in_specs=in_specs,
            out_specs=out_specs,
            check_vma=False,
        )(grad_out, expert_ids, probs, hidden, weights, momentum)

    return program
```

```python
import functools
import math

import jax
import jax.numpy as jnp
from jax import lax
from jax.experimental import pallas as pl
from jax.experimental.pallas import tpu as pltpu
from jax.sharding import PartitionSpec as P

EXP_DEV = 4
ITERS = 5


momentum_decay = 0.95
coef_a = 3.4445
coef_b = -4.775
coef_c = 2.0315


def orthogonal(matrix):
    values = matrix.astype(jnp.float32)
    frob_norm = jnp.sqrt(jnp.sum(values * values))
    iterate = (values / (frob_norm + 1e-07)).astype(jnp.bfloat16)
    for step_index in range(ITERS):
        gram_matrix = jnp.dot(iterate, iterate.T, preferred_element_type=jnp.float32).astype(
            jnp.bfloat16
        )
        gram_square = jnp.dot(gram_matrix, gram_matrix, preferred_element_type=jnp.float32)
        poly_mix = (coef_b * gram_matrix.astype(jnp.float32) + coef_c * gram_square).astype(
            jnp.bfloat16
        )
        iterate = (
            coef_a * iterate.astype(jnp.float32)
            + jnp.dot(poly_mix, iterate, preferred_element_type=jnp.float32)
        ).astype(jnp.bfloat16)
    return iterate.astype(jnp.float32) * math.sqrt(matrix.shape[1])


def scale_rows(prob_slots, grad_slots):
    return (prob_slots[..., None].astype(jnp.float32) * grad_slots.astype(jnp.float32)).astype(
        jnp.bfloat16
    )


def shards(grad_out, expert_ids, probs, hidden, weights, momentum):
    tok_rows, model_width = grad_out.shape
    top_count = expert_ids.shape[1]
    hidden_width = hidden.shape[2]
    owner_count = lax.axis_size("expert")
    expert_total = EXP_DEV * owner_count
    capacity = 2 * tok_rows * top_count // expert_total
    routed_rows = tok_rows * top_count
    flat_ids = expert_ids.reshape(-1)
    onehot = (flat_ids[:, None] == jnp.arange(expert_total, dtype=jnp.int32)[None, :]).astype(
        jnp.int32
    )
    before = jnp.cumsum(onehot, 0) - onehot
    position_in = jnp.sum(before * onehot, 1)
    owner_rank = flat_ids // EXP_DEV
    local_index = flat_ids % EXP_DEV
    buffer_index = (local_index * owner_count + owner_rank) * capacity + position_in
    source_map = (
        jnp.zeros((expert_total * capacity,), jnp.int32)
        .at[buffer_index]
        .set(jnp.arange(routed_rows, dtype=jnp.int32) + 1)
    )
    filled = source_map > 0
    source_row = jnp.maximum(source_map - 1, 0)
    hidden_flat = hidden.reshape(routed_rows, hidden_width)
    prob_flat = probs.reshape(-1)
    zero_value = jnp.zeros((), jnp.bfloat16)
    send_grad = jnp.where(filled[:, None], grad_out[source_row // top_count], zero_value).reshape(
        EXP_DEV, owner_count, capacity, model_width
    )
    send_hidden = jnp.where(filled[:, None], hidden_flat[source_row], zero_value).reshape(
        EXP_DEV, owner_count, capacity, hidden_width
    )
    send_prob = jnp.where(filled, prob_flat[source_row], zero_value).reshape(
        EXP_DEV, owner_count, capacity
    )
    recv_grad, recv_hidden, recv_prob = (
        lax.all_to_all(send_grad, "expert", split_axis=1, concat_axis=1, tiled=True),
        lax.all_to_all(send_hidden, "expert", split_axis=1, concat_axis=1, tiled=True),
        lax.all_to_all(send_prob, "expert", split_axis=1, concat_axis=1, tiled=True),
    )
    grad_part = recv_grad
    raw_grad = jnp.einsum(
        "escd,efd->escf",
        grad_part,
        lax.all_gather(weights, "dp", axis=0, tiled=True),
        preferred_element_type=jnp.float32,
    ).astype(jnp.bfloat16)
    grad_part = recv_grad
    scaled = scale_rows(recv_prob, grad_part)
    grad_weights = lax.psum_scatter(
        jnp.einsum(
            "escf,escd->efd", recv_hidden, scaled, preferred_element_type=jnp.float32
        ).astype(jnp.bfloat16),
        "dp",
        scatter_dimension=0,
        tiled=True,
    ).astype(jnp.float32)
    returned = lax.all_to_all(raw_grad, "expert", split_axis=1, concat_axis=1, tiled=True)
    raw_rows = returned.reshape(expert_total * capacity, hidden_width)[buffer_index]
    grad_hidden = (prob_flat[:, None].astype(jnp.float32) * raw_rows.astype(jnp.float32)).astype(
        jnp.bfloat16
    )
    grad_prob = jnp.sum(raw_rows.astype(jnp.float32) * hidden_flat.astype(jnp.float32), 1)
    new_momentum = (momentum_decay * momentum.astype(jnp.float32) + grad_weights).astype(
        jnp.bfloat16
    )
    update = jax.vmap(orthogonal)(new_momentum)
    return (
        grad_hidden.reshape(tok_rows, top_count, hidden_width),
        grad_prob.reshape(tok_rows, top_count),
        new_momentum,
        update,
    )


def exchange_kernel(
    owners,
    width,
    grad_ref,
    hid_ref,
    weight_ref,
    all_ref,
    recv_ref,
    raw_ref,
    rows_ref,
    local_sem,
    up_sem,
    down_sem,
    cross_sem,
    sib_sem,
    block_sem,
    hid_send,
    hid_recv,
):
    total = owners * width
    row = lax.axis_index("expert")
    lane = lax.axis_index("dp")
    sibling = lane + 1 - 2 * lax.rem(lane, 2)
    cross = lax.rem(lane + 2, width)
    cross_sibling = lax.rem(sibling + 2, width)
    me = row * width + lane

    def target(peer_row, peer_lane):
        return {"expert": peer_row, "dp": peer_lane}

    def peer_at(offset):
        return lax.rem(me + offset, total)

    barrier = pltpu.get_barrier_semaphore()

    @pl.loop(1, total)
    def _(offset):
        peer = peer_at(offset)
        pl.semaphore_signal(
            barrier,
            inc=1,
            device_id=target(peer // width, lax.rem(peer, width)),
            device_id_type=pl.DeviceIdType.MESH,
        )

    pl.semaphore_wait(barrier, total - 1)

    def block_copy(source_row, source_lane, send_sem, peer_row, peer_lane, first=False):
        rank = source_row * width + source_lane
        return pltpu.make_async_remote_copy(
            src_ref=grad_ref if first else all_ref.at[rank],
            dst_ref=all_ref.at[rank],
            send_sem=send_sem,
            recv_sem=block_sem.at[rank],
            device_id=target(peer_row, peer_lane),
            device_id_type=pl.DeviceIdType.MESH,
        )

    def up(source_row, first=False):
        return block_copy(source_row, lane, up_sem.at[source_row], row + 1, lane, first)

    def down(source_row, first=False):
        return block_copy(source_row, lane, down_sem.at[source_row], row - 1, lane, first)

    def over(source_row, first=False):
        return block_copy(source_row, lane, cross_sem.at[source_row], row, cross, first)

    def aside(source_row, column, first=False):
        source_lane = cross if column else lane
        return block_copy(
            source_row, source_lane, sib_sem.at[source_row * 2 + column], row, sibling, first
        )

    def arrive(source_row, source_lane):
        block_copy(source_row, source_lane, up_sem.at[0], row, sibling).wait_recv()

    def hid_copy(offset):
        peer = peer_at(offset)
        return pltpu.make_async_remote_copy(
            src_ref=hid_ref.at[peer],
            dst_ref=recv_ref.at[me],
            send_sem=hid_send.at[offset],
            recv_sem=hid_recv.at[me],
            device_id=target(peer // width, lax.rem(peer, width)),
            device_id_type=pl.DeviceIdType.MESH,
        )

    @pl.when(row < owners - 1)
    def _():
        up(row, True).start()

    @pl.when(row > 0)
    def _():
        down(row, True).start()

    over(row, True).start()
    aside(row, 0, True).start()
    own_grad = pltpu.make_async_copy(grad_ref, all_ref.at[me], local_sem.at[0])
    own_grad.start()
    own_hid = pltpu.make_async_copy(hid_ref.at[me], recv_ref.at[me], local_sem.at[1])
    own_hid.start()

    def start_hidden(low, high):
        @pl.loop(low, high)
        def _(offset):
            hid_copy(offset).start()

    first_batch = 1 + (total - 1) // 3

    def cross_arrival(source_row):
        arrive(source_row, cross)
        aside(source_row, 1).start()

    for step in range(1, owners + 1):
        if step < owners:

            @pl.when(row - step >= 0)
            def _():
                arrive(row - step, lane)

                @pl.when(row < owners - 1)
                def _():
                    up(row - step).start()

                over(row - step).start()
                aside(row - step, 0).start()

            @pl.when(row + step < owners)
            def _():
                arrive(row + step, lane)

                @pl.when(row > 0)
                def _():
                    down(row + step).start()

                over(row + step).start()
                aside(row + step, 0).start()

        if step == 1:
            start_hidden(1, first_batch)
        elif step == 2:
            start_hidden(first_batch, total)

        if step == 1:
            cross_arrival(row)
        else:

            @pl.when(row - (step - 1) >= 0)
            def _():
                cross_arrival(row - (step - 1))

            @pl.when(row + (step - 1) < owners)
            def _():
                cross_arrival(row + (step - 1))

    own_grad.wait()
    own_hid.wait()

    @pl.loop(0, owners)
    def _(source_row):
        arrive(source_row, sibling)
        arrive(source_row, cross_sibling)
        load = pltpu.make_async_copy(
            all_ref.at[pl.ds(source_row * width, width)], rows_ref, local_sem.at[0]
        )
        load.start()
        load.wait()
        for place in range(width):
            raw_ref[source_row * width + place] = lax.dot_general(
                rows_ref[place],
                weight_ref[...],
                (((1,), (1,)), ((), ())),
                preferred_element_type=jnp.float32,
            ).astype(raw_ref.dtype)
        over(source_row).wait_send()
        aside(source_row, 0).wait_send()
        aside(source_row, 1).wait_send()

        @pl.when((source_row <= row) & (row < owners - 1))
        def _():
            up(source_row).wait_send()

        @pl.when((source_row >= row) & (row > 0))
        def _():
            down(source_row).wait_send()

    @pl.loop(1, total)
    def _(offset):
        hid_copy(offset).wait_send()
        peer = peer_at(offset)
        pltpu.make_async_remote_copy(
            src_ref=hid_ref.at[peer],
            dst_ref=recv_ref.at[peer],
            send_sem=hid_send.at[offset],
            recv_sem=hid_recv.at[peer],
            device_id=target(peer // width, lax.rem(peer, width)),
            device_id_type=pl.DeviceIdType.MESH,
        ).wait_recv()


def exchange(grad_out, send_hidden, weight):
    owners, width = lax.axis_size("expert"), lax.axis_size("dp")
    total = owners * width
    dma = pltpu.SemaphoreType.DMA
    return pl.pallas_call(
        functools.partial(exchange_kernel, owners, width),
        out_shape=(
            jax.ShapeDtypeStruct((total,) + grad_out.shape, grad_out.dtype),
            jax.ShapeDtypeStruct(send_hidden.shape, send_hidden.dtype),
            jax.ShapeDtypeStruct(send_hidden.shape, send_hidden.dtype),
        ),
        in_specs=[pl.BlockSpec(memory_space=pl.ANY)] * 2 + [pl.BlockSpec(memory_space=pltpu.VMEM)],
        out_specs=(pl.BlockSpec(memory_space=pl.ANY),) * 2
        + (pl.BlockSpec(memory_space=pltpu.VMEM),),
        scratch_shapes=[
            pltpu.VMEM((width,) + grad_out.shape, grad_out.dtype),
            dma((2,)),
            dma((owners,)),
            dma((owners,)),
            dma((owners,)),
            dma((2 * owners,)),
            dma((total,)),
            dma((total,)),
            dma((total,)),
        ],
        compiler_params=pltpu.CompilerParams(collective_id=0, has_side_effects=True, vmem_limit_bytes=24 * 2**20),
        name="exchange",
    )(grad_out, send_hidden, weight)


def orthogonal_kernel(tiles, momentum_ref, update_ref, iterate_ref):
    height, width = momentum_ref.shape
    columns = width // tiles

    def tile(index):
        return pl.ds(pl.multiple_of(index * columns, columns), columns)

    def add_squares(index, total):
        values = momentum_ref[:, tile(index)].astype(jnp.float32)
        return total + jnp.sum(values * values, axis=0, keepdims=True)

    squares = lax.fori_loop(0, tiles, add_squares, jnp.zeros((1, columns), jnp.float32))
    frob_norm = jnp.sqrt(jnp.sum(squares, axis=1, keepdims=True)) + 1e-07

    @pl.loop(0, tiles)
    def _(index):
        values = momentum_ref[:, tile(index)].astype(jnp.float32)
        iterate_ref[:, tile(index)] = (values / frob_norm).astype(jnp.bfloat16)

    @pl.loop(0, ITERS)
    def _(step_index):
        iterate = iterate_ref[...]
        gram_matrix = lax.dot_general(
            iterate, iterate, (((1,), (1,)), ((), ())), preferred_element_type=jnp.float32
        ).astype(jnp.bfloat16)
        gram_square = jnp.dot(gram_matrix, gram_matrix, preferred_element_type=jnp.float32)
        poly_mix = (coef_b * gram_matrix.astype(jnp.float32) + coef_c * gram_square).astype(
            jnp.bfloat16
        )
        for index in range(tiles):
            part = pl.ds(index * columns, columns)
            block = iterate_ref[:, part]
            iterate_ref[:, part] = (
                coef_a * block.astype(jnp.float32)
                + jnp.dot(poly_mix, block, preferred_element_type=jnp.float32)
            ).astype(jnp.bfloat16)

    @pl.loop(0, tiles)
    def _(index):
        update_ref[:, tile(index)] = iterate_ref[:, tile(index)].astype(jnp.float32) * math.sqrt(
            width
        )


def orthogonal_block(matrix):
    height, width = matrix.shape
    macs = ITERS * height * height * (2 * width + height)
    return pl.pallas_call(
        functools.partial(orthogonal_kernel, width // 512),
        out_shape=jax.ShapeDtypeStruct(matrix.shape, jnp.float32),
        in_specs=[pl.BlockSpec(memory_space=pltpu.VMEM)],
        out_specs=pl.BlockSpec(memory_space=pltpu.VMEM),
        scratch_shapes=[pltpu.VMEM(matrix.shape, jnp.bfloat16)],
        compiler_params=pltpu.CompilerParams(vmem_limit_bytes=24 * 2**20),
        cost_estimate=pl.CostEstimate(
            flops=2 * macs, bytes_accessed=6 * height * width, transcendentals=0
        ),
        name="orthogonal",
    )(matrix)


def dense_shards(grad_out, expert_ids, probs, hidden, weights, momentum):
    axes = ("expert", "dp")
    tok_rows, model_width = grad_out.shape
    top_count = expert_ids.shape[1]
    hidden_width = hidden.shape[2]
    device_count = lax.axis_size("expert") * lax.axis_size("dp")
    expert_total = device_count * weights.shape[0]
    experts = jnp.arange(expert_total, dtype=jnp.int32)
    zero_value = jnp.zeros((), jnp.bfloat16)
    prob_hidden = (probs[..., None].astype(jnp.float32) * hidden.astype(jnp.float32)).astype(
        jnp.bfloat16
    )
    send_hidden = jnp.zeros((expert_total, tok_rows, hidden_width), jnp.bfloat16)
    for choice in range(top_count):
        named = expert_ids[None, :, choice] == experts[:, None]
        send_hidden = jnp.where(named[..., None], prob_hidden[None, :, choice], send_hidden)
    all_grad, recv_hidden, raw_grad = exchange(grad_out, send_hidden, weights[0])
    all_grad = all_grad.reshape(device_count * tok_rows, model_width)
    returned = lax.all_to_all(
        raw_grad,
        axes,
        split_axis=0,
        concat_axis=0,
        tiled=True,
    )
    grad_weights = lax.dot_general(
        recv_hidden.reshape(device_count * tok_rows, hidden_width),
        all_grad,
        (((0,), (0,)), ((), ())),
        preferred_element_type=jnp.float32,
    )[None]
    new_momentum = (momentum_decay * momentum.astype(jnp.float32) + grad_weights).astype(
        jnp.bfloat16
    )
    update = orthogonal_block(new_momentum[0])[None]
    update, returned = lax.optimization_barrier((update, returned))
    raw_rows = jnp.zeros((tok_rows, top_count, hidden_width), jnp.bfloat16)
    for expert in range(expert_total):
        named = expert_ids == expert
        raw_rows = jnp.where(named[..., None], returned[expert][:, None], raw_rows)
    grad_hidden = (probs[..., None].astype(jnp.float32) * raw_rows.astype(jnp.float32)).astype(
        jnp.bfloat16
    )
    grad_prob = jnp.sum(raw_rows.astype(jnp.float32) * hidden.astype(jnp.float32), 2)
    return grad_hidden, grad_prob, new_momentum, update


def solution(mesh):
    in_specs = (
        P(("group", "expert", "dp"), None),
        P(("group", "expert", "dp"), None),
        P(("group", "expert", "dp"), None),
        P(("group", "expert", "dp"), None, None),
        P(("expert", "dp"), None, None),
        P(("group", "expert", "dp"), None, None),
    )
    out_specs = (
        P(("group", "expert", "dp"), None, None),
        P(("group", "expert", "dp"), None),
        P(("group", "expert", "dp"), None, None),
        P(("group", "expert", "dp"), None, None),
    )

    owners = mesh.shape["expert"]
    dp_count = mesh.shape["dp"]

    def program(grad_out, expert_ids, probs, hidden, weights, momentum):
        tok_rows = grad_out.shape[0] // (mesh.shape["group"] * owners * dp_count)
        expert_total = weights.shape[0]
        dense = owners >= 3 and dp_count == 4 and expert_total == owners * dp_count and (
            2 * tok_rows * expert_ids.shape[1] // expert_total >= tok_rows
        )
        return jax.shard_map(
            dense_shards if dense else shards,
            mesh=mesh,
            in_specs=in_specs,
            out_specs=out_specs,
            check_vma=False,
        )(grad_out, expert_ids, probs, hidden, weights, momentum)

    return program
```
